32 devices in a mesh: groups: 2 (over y), ep: 4 (over z), tp: 2 (over x), sp: 2 (over core).
Axes of the slice: x: 2, y: 2, z: 4, core: 2. Of those that a mesh axis runs over, the one named last changes fastest.
Arguments:
- logits: float32 [2048, 128], P(('groups', 'ep', 'sp')), parts along dimension 0, may hold values from -30 to 410
- routes: int32 [2048, 8], P(('groups', 'ep', 'sp')), parts along dimension 0, may hold values from 0 to 127, as said below
- owner: int32 [2048], P(('groups', 'ep', 'sp')), parts along dimension 0, may hold values from 0 to 1023, as said below
- tokens: bfloat16 [2048, 4096], P(('groups', 'ep', 'sp')), parts along dimension 0, may hold values from -6 to 6
- out_grad: bfloat16 [2048, 4096], P(('groups', 'ep', 'sp')), parts along dimension 0, may hold values from -6 to 6
- resp_lengths: int32 [16], P(('groups', 'ep', 'sp')), parts along dimension 0, may hold values from 1 to 128
- w_gate: bfloat16 [4, 4096, 1536], P('ep', None, 'tp'), may hold values from -0.09375 to 0.09375
- w_up: bfloat16 [4, 4096, 1536], P('ep', None, 'tp'), may hold values from -0.09375 to 0.09375
- w_down: bfloat16 [4, 1536, 4096], P('ep', 'tp'), may hold values from -0.15625 to 0.15625
Outputs:
- layer_out: bfloat16 [2048, 4096], P(('groups', 'ep', 'sp'), 'tp'), parts along dimension 0
- token_grad: bfloat16 [2048, 4096], P(('groups', 'ep', 'sp'), 'tp'), parts along dimension 0
- router_grad: float32 [2048, 128], P(('groups', 'ep', 'sp')), parts along dimension 0
The draws below stay inside these ranges and needn't reach their ends.
There are 2 independent parts, one for each index of `groups`. The reference program is written for one: setup_inputs(seed, part) draws one part's arguments, and reference() takes and returns one part's arrays. A program takes and returns all parts, laid end to end along the dimension named above; an argument that names none is the same for every part. Nothing has to cross between parts.
Inputs may be any that keep to these rules, and one draw needn't show every extreme that they name: owner is a permutation of the group's 1024 token positions. Of the 128 rows of one device (aligned blocks in rollout order) at most 32 go to the 128 tokens of one owner (aligned blocks in learner order), and some such pair reaches 32. `routes`: each row names 8 different experts, exactly one of them below 4. Among the 128 tokens of any one owner (the rows that `owner` maps into that owner's block), no expert below 4 is named by more than 64 of them, and for every owner some expert below 4 is named by exactly 64.
All inputs are finite; a program needn't handle non-finite values.
Results may differ from the reference program's by a relative error of at most 0.0095.
Values may be sent and summed in bfloat16 or wider, within the bound.
A program may use at most 128 MiB of HBM per device.

```python
import jax
import jax.numpy as jnp
from jax import lax

D = 4096
FF = 1536
ROUTER = 128
TOP = 8
TOK_DEV = 128
EXPERTS = 4
OWNERS = 8
TOKENS = 1024
CAP = 64
N_TP = 2


def owner_table(key):
    share = TOK_DEV // OWNERS
    keys = jax.random.split(key, 6)
    upper = jax.random.randint(keys[0], (OWNERS // 2,), 0, share + 1).astype(jnp.int32).at[0].set(share)
    offsets = jax.random.permutation(keys[1], jnp.concatenate([upper, -upper]))
    sources = jax.random.permutation(keys[2], OWNERS)
    targets = jax.random.permutation(keys[3], OWNERS)
    counts = share + offsets[(targets[None, :] + sources[:, None]) % OWNERS]
    ends = jnp.cumsum(counts, axis=1)
    steps_seen = jnp.arange(TOK_DEV, dtype=jnp.int32)
    target_of = jnp.sum((ends[:, None, :] <= steps_seen[None, :, None]).astype(jnp.int32), axis=2)
    within = steps_seen[None, :] - jnp.take_along_axis(ends - counts, target_of, axis=1)
    before = jnp.cumsum(counts, axis=0) - counts
    arrival = jnp.take_along_axis(before, target_of, axis=1) + within
    learner_perm = jax.vmap(lambda sub_key: jax.random.permutation(sub_key, TOK_DEV))(jax.random.split(keys[4], OWNERS))
    learner = target_of * TOK_DEV + learner_perm[target_of, arrival]
    rollout_perm = jax.vmap(lambda sub_key: jax.random.permutation(sub_key, TOK_DEV))(jax.random.split(keys[5], OWNERS))
    rollout = jnp.arange(OWNERS, dtype=jnp.int32)[:, None] * TOK_DEV + rollout_perm
    return jnp.zeros((TOKENS,), jnp.int32).at[rollout.reshape(-1)].set(learner.reshape(-1).astype(jnp.int32))


def route_table(key):
    keys = jax.random.split(key, 6)
    slot_count = EXPERTS * CAP
    hottest = jax.random.randint(keys[0], (), 0, EXPERTS)
    second = (hottest + 1 + jax.random.randint(keys[1], (OWNERS,), 0, EXPERTS - 1)) % EXPERTS
    odd_block = jnp.arange(OWNERS) % 2 == 1
    line = jnp.arange(slot_count, dtype=jnp.int32)
    slot_ids = line // CAP
    noise = jax.random.randint(keys[2], (OWNERS, slot_count), 0, 2 ** 18)
    ranking = (noise + 1) * slot_count + line[None, :]
    ranking = jnp.where(odd_block[:, None] & (slot_ids[None, :] == second[:, None]), line[None, :] - slot_count, ranking)
    ranking = jnp.where(slot_ids[None, :] == hottest, line[None, :] - 2 * slot_count, ranking)
    chosen = jnp.argsort(ranking, axis=1)[:, :TOK_DEV]
    window = slot_ids[chosen]
    shuffle = jax.vmap(lambda sub_key: jax.random.permutation(sub_key, TOK_DEV))(jax.random.split(keys[3], OWNERS))
    window = jnp.take_along_axis(window, shuffle, axis=1).reshape(-1)
    columns = jnp.arange(ROUTER, dtype=jnp.int32)
    others_rank = jax.random.randint(keys[4], (TOKENS, ROUTER), 0, 2 ** 18) * ROUTER + columns[None, :]
    others_rank = jnp.where(columns[None, :] < EXPERTS, -1, others_rank)
    others = jnp.argsort(-others_rank, axis=1)[:, :TOP - 1].astype(jnp.int32)
    place_at = jax.random.randint(keys[5], (TOKENS,), 0, TOP)
    column = jnp.arange(TOP, dtype=jnp.int32)[None, :]
    source_col = jnp.clip(jnp.where(column < place_at[:, None], column, column - 1), 0, TOP - 2)
    filled = jnp.take_along_axis(others, source_col, axis=1)
    return jnp.where(column == place_at[:, None], window[:, None], filled).astype(jnp.int32)


def draw_owner(key, part):
    return owner_table(key)


def draw_routes(key, part):
    owner_map = owner_table(key)
    key = jax.random.fold_in(key, 5)
    in_learner = route_table(key)
    return in_learner[owner_map]


def draw_logits(key, part):
    key = jax.random.fold_in(key, 9)
    keys = jax.random.split(key, 1)
    return jnp.clip(0.4 * jax.random.normal(keys[0], (TOKENS, ROUTER), jnp.float32), -2.4, 2.4)


def place_ends(result, key, low, largest):
    longest = result.shape.index(max(result.shape))
    spots = []
    for shift in (0, 1):
        where = [jax.random.randint(jax.random.fold_in(key, axis), (), 0, length) for axis, length in enumerate(result.shape)]
        where[longest] = (where[longest] + shift) % result.shape[longest]
        spots.append(tuple(where))
    return result.at[spots[0]].set(low).at[spots[1]].set(largest)


def shard_levels(stream_key, dims, cuts, smallest, top_value):
    loudness, own = 1.0, jax.random.fold_in(stream_key, 6)
    for dim, shards_of in cuts:
        draws = jnp.exp(jax.random.uniform(jax.random.fold_in(own, dim), (shards_of,), jnp.float32, smallest / len(cuts), top_value / len(cuts)))
        loudness = loudness * jnp.repeat(draws, dims[dim] // shards_of).reshape([-1 if axis == dim else 1 for axis in range(len(dims))])
    return loudness


def bell_draw(stream_key, dims, deviation, most, shards=(), held_as=jnp.bfloat16):
    values = jax.random.normal(stream_key, dims, jnp.float32) * deviation
    if len(shards) > 0:
        values = shard_levels(stream_key, dims, shards, -0.22, 0.18) * values
    return jnp.clip(values, min=-most, max=most).astype(held_as)


def setup_inputs(seed: int = 0, part: int = 0) -> dict:
    arg_keys = jax.random.split(jax.random.key(seed), 10)
    own_keys = jax.random.split(jax.random.fold_in(arg_keys[9], part), 10)
    logits = draw_logits(jax.random.fold_in(jax.random.fold_in(arg_keys[9], part), 71), part)
    routes = draw_routes(jax.random.fold_in(jax.random.fold_in(arg_keys[9], part), 71), part)
    owner = draw_owner(jax.random.fold_in(jax.random.fold_in(arg_keys[9], part), 71), part)
    tokens = bell_draw(own_keys[3], (TOKENS, D), 1.0, 6.0, ((0, 8),))
    out_grad = bell_draw(own_keys[4], (TOKENS, D), 1.0, 6.0, ((0, 8),))
    resp_lengths = place_ends(jax.random.randint(own_keys[5], (OWNERS,), 1, TOK_DEV + 1), jax.random.fold_in(own_keys[5], 1), 1, TOK_DEV).astype(jnp.int32)
    w_gate = bell_draw(arg_keys[6], (EXPERTS, D, FF), D ** -0.5, 0.09375, ((0, 4), (2, 2)))
    w_up = bell_draw(arg_keys[7], (EXPERTS, D, FF), D ** -0.5, 0.09375, ((0, 4), (2, 2)))
    w_down = bell_draw(arg_keys[8], (EXPERTS, FF, D), FF ** -0.5, 0.15625, ((0, 4), (1, 2)))
    return dict(logits=logits, routes=routes, owner=owner, tokens=tokens, out_grad=out_grad, resp_lengths=resp_lengths, w_gate=w_gate, w_up=w_up, w_down=w_down)


def softmax_rows(values):
    highest = jnp.max(values, axis=1, keepdims=True)
    raised = jnp.exp(values - highest)
    return raised / jnp.sum(raised, axis=1, keepdims=True)


def block_round(values):
    return lax.optimization_barrier(values.astype(jnp.bfloat16)).astype(jnp.float32)


def reference(logits, routes, owner, tokens, out_grad, resp_lengths, w_gate, w_up, w_down):
    learner_logits = jnp.zeros_like(logits).at[owner].set(logits)
    learner_routes = jnp.zeros_like(routes).at[owner].set(routes)
    picked = jnp.take_along_axis(learner_logits, learner_routes, axis=1)
    gate_weights = softmax_rows(picked)
    in_window = learner_routes < EXPERTS
    expert_ids = jnp.sum(jnp.where(in_window, learner_routes, 0), axis=1).astype(jnp.int32)
    weight = jnp.sum(jnp.where(in_window, gate_weights, 0.0), axis=1)
    weight_b = weight.astype(jnp.bfloat16)
    positions = jnp.arange(TOKENS, dtype=jnp.int32)
    live_mask = (positions % TOK_DEV) < resp_lengths[positions // TOK_DEV]
    masked_grad = jnp.where(live_mask[:, None], out_grad, jnp.zeros_like(out_grad))
    padded_tokens = jnp.concatenate([tokens, jnp.zeros((1, D), tokens.dtype)], axis=0)
    padded_grad = jnp.concatenate([masked_grad, jnp.zeros((1, D), masked_grad.dtype)], axis=0)
    padded_weight = jnp.concatenate([weight_b, jnp.zeros((1,), weight_b.dtype)], axis=0)
    capacity = OWNERS * CAP
    block_width = FF // N_TP

    def one_expert(expert):
        row_ids = jnp.nonzero(expert_ids == expert, size=capacity, fill_value=TOKENS)[0].astype(jnp.int32)
        inputs = padded_tokens[row_ids]
        grad_in = padded_grad[row_ids]
        gate_scale = padded_weight[row_ids].astype(jnp.float32)
        gate_mat = w_gate[expert]
        up_mat = w_up[expert]
        down_mat = w_down[expert]
        pre_gate = jnp.dot(inputs, gate_mat, preferred_element_type=jnp.float32)
        pre_up = jnp.dot(inputs, up_mat, preferred_element_type=jnp.float32)
        down_back = jnp.dot(grad_in, down_mat.T, preferred_element_type=jnp.float32)
        gate_sigmoid = jax.nn.sigmoid(pre_gate)
        active = pre_gate * gate_sigmoid
        hidden = (active * pre_up).astype(jnp.bfloat16)
        hidden_blocks = hidden.astype(jnp.float32).reshape(capacity, N_TP, block_width)
        down_blocks = down_mat.astype(jnp.float32).reshape(N_TP, block_width, D)
        out_terms = jnp.einsum("mqf,qfd->mqd", hidden_blocks, down_blocks) * gate_scale[:, None, None]
        out_rows = jnp.sum(block_round(out_terms), axis=1).astype(jnp.bfloat16)
        score_terms = jnp.sum((hidden.astype(jnp.float32) * down_back).reshape(capacity, N_TP, block_width), axis=2)
        score_rows = jnp.sum(block_round(score_terms), axis=1).astype(jnp.bfloat16)
        grad_hidden = gate_scale[:, None] * down_back
        grad_up = (grad_hidden * active).astype(jnp.bfloat16)
        grad_gate = (grad_hidden * pre_up * (gate_sigmoid * (1.0 + pre_gate * (1.0 - gate_sigmoid)))).astype(jnp.bfloat16)
        gate_blocks = gate_mat.astype(jnp.float32).reshape(D, N_TP, block_width)
        up_blocks = up_mat.astype(jnp.float32).reshape(D, N_TP, block_width)
        grad_terms = jnp.einsum("mqf,dqf->mqd", grad_gate.astype(jnp.float32).reshape(capacity, N_TP, block_width), gate_blocks)
        grad_terms = grad_terms + jnp.einsum("mqf,dqf->mqd", grad_up.astype(jnp.float32).reshape(capacity, N_TP, block_width), up_blocks)
        grad_rows = jnp.sum(block_round(grad_terms), axis=1).astype(jnp.bfloat16)
        return out_rows, grad_rows, score_rows, row_ids

    out_all, grad_all, score_all, rows_all = lax.map(one_expert, jnp.arange(EXPERTS, dtype=jnp.int32))
    targets = rows_all.reshape(-1)
    layer_out = jnp.zeros((TOKENS + 1, D), jnp.bfloat16).at[targets].set(out_all.reshape(-1, D))[:TOKENS]
    token_grad = jnp.zeros((TOKENS + 1, D), jnp.bfloat16).at[targets].set(grad_all.reshape(-1, D))[:TOKENS]
    token_score = jnp.zeros((TOKENS + 1,), jnp.bfloat16).at[targets].set(score_all.reshape(-1))[:TOKENS].astype(jnp.float32)
    route_grad = token_score[:, None] * weight[:, None] * (in_window.astype(jnp.float32) - gate_weights)
    columns = jnp.arange(ROUTER, dtype=jnp.int32)
    router_grad = jnp.sum(jnp.where(learner_routes[:, :, None] == columns[None, None, :], route_grad[:, :, None], 0.0), axis=1)
    return layer_out, token_grad, router_grad
```

```python
import functools

import jax
import jax.numpy as jnp
from jax import lax
from jax.experimental import pallas as pl
from jax.experimental.pallas import tpu as pltpu
from jax.sharding import PartitionSpec as P

MESH = pl.DeviceIdType.MESH
LANES = 128


def dot_nn(left, right):
    return jnp.dot(left, right, preferred_element_type=jnp.float32)


def dot_nt(left, right):
    return lax.dot_general(
        left, right, (((1,), (1,)), ((), ())), preferred_element_type=jnp.float32
    )


def layer_kernel(
    ep,
    tp,
    per,
    pack_ref,
    pack_grad_ref,
    unpack_ref,
    weight_ref,
    coef_ref,
    tokens_ref,
    grads_ref,
    gate_hbm,
    up_hbm,
    down_hbm,
    out_ref,
    token_grad_ref,
    router_ref,
    w_gate,
    w_up,
    w_down,
    tok_send,
    grad_send,
    tok_all,
    grad_all,
    pre_gate,
    pre_up,
    hidden,
    out_part,
    out_recv,
    out_back,
    out_home,
    tg_part,
    tg_recv,
    tg_back,
    tg_home,
    w_sem,
    z_send,
    z_recv,
    x_send,
    x_recv,
):
    share = tok_send.shape[2]
    z = lax.axis_index("ep")
    x = lax.axis_index("tp")

    def rows_of(index):
        return pl.ds(pl.multiple_of(index * per, per), per)

    def source(k):
        return lax.rem(z - k + ep, ep)

    def holder(k):
        return lax.rem(z + k, ep)

    barrier = pltpu.get_barrier_semaphore()
    for k in range(1, ep):
        pl.semaphore_signal(barrier, inc=1, device_id={"ep": holder(k)}, device_id_type=MESH)
    for j in range(1, tp):
        pl.semaphore_signal(
            barrier, inc=1, device_id={"tp": lax.rem(x + j, tp)}, device_id_type=MESH
        )

    w_copies = [
        pltpu.make_async_copy(gate_hbm.at[0], w_gate, w_sem.at[0]),
        pltpu.make_async_copy(up_hbm.at[0], w_up, w_sem.at[1]),
        pltpu.make_async_copy(down_hbm.at[0], w_down, w_sem.at[2]),
    ]
    for copy in w_copies:
        copy.start()

    def z_copy(kind, k):
        if kind < 2:
            sent, landed = ((tok_send, tok_all), (grad_send, grad_all))[kind]
            return pltpu.make_async_remote_copy(
                src_ref=sent.at[k],
                dst_ref=landed.at[x, rows_of(z)],
                send_sem=z_send.at[kind, k],
                recv_sem=z_recv.at[kind, k],
                device_id={"ep": holder(k)},
                device_id_type=MESH,
            )
        sent, landed = ((out_back, out_home), (tg_back, tg_home))[kind - 2]
        return pltpu.make_async_remote_copy(
            src_ref=sent.at[rows_of(source(k))],
            dst_ref=landed.at[rows_of(z)],
            send_sem=z_send.at[kind, k],
            recv_sem=z_recv.at[kind, k],
            device_id={"ep": source(k)},
            device_id_type=MESH,
        )

    def x_copy(kind, k, j):
        rows = rows_of(source(k))
        target = lax.rem(x + j, tp)
        if kind < 2:
            buffer = (tok_all, grad_all)[kind]
            sent, landed = buffer.at[x, rows], buffer.at[x, rows]
        else:
            part, recv = ((out_part, out_recv), (tg_part, tg_recv))[kind - 2]
            sent, landed = part.at[target, rows], recv.at[j - 1, rows]
        return pltpu.make_async_remote_copy(
            src_ref=sent,
            dst_ref=landed,
            send_sem=x_send.at[kind, k * tp + j],
            recv_sem=x_recv.at[kind, k * tp + j],
            device_id={"tp": target},
            device_id_type=MESH,
        )

    def x_start(kind, k):
        for j in range(1, tp):
            x_copy(kind, k, j).start()

    def x_wait_recv(kind, k):
        for j in range(1, tp):
            x_copy(kind, k, j).wait_recv()

    mine = pl.ds(pl.multiple_of(x * share, LANES), share)
    pl.semaphore_wait(barrier, ep - 1 + tp - 1)

    @pl.loop(1, ep)
    def _(k):
        packed = dot_nn(pack_ref[rows_of(holder(k)), :], tokens_ref[:, mine])
        tok_send[k] = packed.astype(jnp.bfloat16)
        z_copy(0, k).start()

    @pl.loop(0, tp)
    def _(h):
        lanes = pl.ds(pl.multiple_of(h * share, LANES), share)
        tok_all[h, rows_of(z), :] = dot_nn(
            pack_ref[rows_of(z), :], tokens_ref[:, lanes]
        ).astype(jnp.bfloat16)
        grad_all[h, rows_of(z), :] = dot_nn(
            pack_grad_ref[rows_of(z), :], grads_ref[:, lanes]
        ).astype(jnp.bfloat16)

    @pl.loop(1, ep)
    def _(k):
        packed = dot_nn(pack_grad_ref[rows_of(holder(k)), :], grads_ref[:, mine])
        grad_send[k] = packed.astype(jnp.bfloat16)

    def pump(kind, k):
        z_copy(kind, k).wait_recv()
        x_start(kind, k)
        if kind == 0:
            z_copy(1, k).start()

    def reduce_rows(kind, k):
        part, recv, back, home = (
            (out_part, out_recv, out_back, out_home),
            (tg_part, tg_recv, tg_back, tg_home),
        )[kind - 2]
        rows = rows_of(source(k))
        x_wait_recv(kind, k)
        total = part[x, rows, :].astype(jnp.float32)
        for j in range(1, tp):
            total = total + recv[j - 1, rows, :].astype(jnp.float32)
        total = total.astype(jnp.bfloat16)

        @pl.when(k == 0)
        def _():
            home[rows, :] = total

        @pl.when(k > 0)
        def _():
            back[rows, :] = total
            z_copy(kind, k).start()

    for copy in w_copies:
        copy.wait()

    @pl.loop(0, ep)
    def _(k):
        rows = rows_of(source(k))

        @pl.when((k >= 1) & (k + 1 < ep))
        def _():
            pump(0, k + 1)

        @pl.when(k >= 1)
        def _():
            x_wait_recv(0, k)

        gate = jnp.zeros((per, w_gate.shape[1]), jnp.float32)
        up = jnp.zeros((per, w_gate.shape[1]), jnp.float32)
        for h in range(tp):
            block = tok_all[h, rows, :]
            gate = gate + dot_nn(block, w_gate[h * share : (h + 1) * share, :])
            up = up + dot_nn(block, w_up[h * share : (h + 1) * share, :])
        pre_gate[rows, :] = gate
        pre_up[rows, :] = up
        hid = (gate * jax.nn.sigmoid(gate) * up).astype(jnp.bfloat16)
        hidden[rows, :] = hid
        for h in range(tp):
            out_part[h, rows, :] = dot_nn(
                hid, w_down[:, h * share : (h + 1) * share]
            ).astype(jnp.bfloat16)
        x_start(2, k)

        @pl.when(k == 0)
        def _():
            pump(0, k + 1)

    @pl.loop(0, ep)
    def _(k):
        rows = rows_of(source(k))

        @pl.when((k >= 1) & (k + 1 < ep))
        def _():
            pump(1, k + 1)

        @pl.when(k >= 1)
        def _():
            x_wait_recv(1, k)

        back = jnp.zeros((per, w_gate.shape[1]), jnp.float32)
        for h in range(tp):
            back = back + dot_nt(grad_all[h, rows, :], w_down[:, h * share : (h + 1) * share])
        gate = pre_gate[rows, :]
        up = pre_up[rows, :]
        sig = jax.nn.sigmoid(gate)
        score = jnp.sum(hidden[rows, :].astype(jnp.float32) * back, axis=1, keepdims=True)
        score = jnp.broadcast_to(score, (per, LANES)).astype(jnp.bfloat16)
        grad_up = (back * (gate * sig)).astype(jnp.bfloat16)
        grad_gate = (back * up * (sig * (1.0 + gate * (1.0 - sig)))).astype(jnp.bfloat16)
        for h in range(tp):
            cols = slice(h * share, (h + 1) * share)
            tg_part[h, rows, 0:share] = (
                dot_nt(grad_gate, w_gate[cols, :]) + dot_nt(grad_up, w_up[cols, :])
            ).astype(jnp.bfloat16)
            tg_part[h, rows, share : share + LANES] = score
        x_start(3, k)
        reduce_rows(2, k)

        @pl.when(k == 0)
        def _():
            pump(1, k + 1)

        @pl.when(k >= 1)
        def _():
            reduce_rows(3, k - 1)

    reduce_rows(3, jnp.int32(ep - 1))

    weight = weight_ref[...]

    @pl.loop(1, ep)
    def _(k):
        z_copy(2, k).wait_recv()

    out_ref[...] = (dot_nn(unpack_ref[...], out_home[...]) * weight).astype(jnp.bfloat16)

    @pl.loop(1, ep)
    def _(k):
        z_copy(3, k).wait_recv()

    token_grad_ref[...] = (
        dot_nn(unpack_ref[...], tg_home[:, 0:share]) * weight
    ).astype(jnp.bfloat16)
    router_ref[...] = (
        dot_nn(unpack_ref[...], tg_home[:, share : share + LANES]) * coef_ref[...]
    )

    for kind in range(4):

        @pl.loop(1, ep)
        def _(k):
            z_copy(kind, k).wait_send()

        @pl.loop(1 if kind < 2 else 0, ep)
        def _(k):
            for j in range(1, tp):
                x_copy(kind, k, j).wait_send()


def shards(logits, routes, owner, tokens, out_grad, resp_lengths, w_gate, w_up, w_down):
    tok_count, width = tokens.shape
    top = routes.shape[1]
    ep = lax.axis_size("ep")
    tp = lax.axis_size("tp")
    sp = lax.axis_size("sp")
    owner_count = ep * sp
    local_count = w_gate.shape[0]
    assert local_count == 1
    hidden_width = w_gate.shape[2]
    per = 2 * tok_count // ep
    slots = ep * per
    share = width // tp
    me = lax.axis_index("ep") * sp + lax.axis_index("sp")

    columns = jnp.arange(logits.shape[1], dtype=jnp.int32)
    hits = routes[:, :, None] == columns[None, None, :]
    picked = jnp.sum(jnp.where(hits, logits[:, None, :], 0.0), axis=2)
    highest = jnp.max(picked, axis=1, keepdims=True)
    raised = jnp.exp(picked - highest)
    gates = raised / jnp.sum(raised, axis=1, keepdims=True)
    table = jnp.concatenate(
        [
            gates.T,
            routes.astype(jnp.float32).T,
            owner.astype(jnp.float32)[None, :],
            jnp.zeros((24 - 2 * top - 1, tok_count), jnp.float32),
        ],
        axis=0,
    )
    everyone = lax.all_gather(table, ("ep", "sp"), axis=1, tiled=True)
    positions = jnp.arange(tok_count, dtype=jnp.float32) + (me * tok_count).astype(jnp.float32)
    chosen = (everyone[2 * top][:, None] == positions[None, :]).astype(jnp.float32)
    mine = jnp.dot(everyone, chosen, precision=lax.Precision.HIGHEST)
    gate_rows = mine[:top]
    route_rows = mine[top : 2 * top]
    in_window = route_rows < ep
    expert_ids = jnp.sum(jnp.where(in_window, route_rows, 0.0), axis=0)
    weight = jnp.sum(jnp.where(in_window, gate_rows, 0.0), axis=0)
    steps = jnp.arange(tok_count, dtype=jnp.int32)
    live = steps < resp_lengths[0]
    same = (expert_ids[:, None] == expert_ids[None, :]) & (steps[:, None] < steps[None, :])
    rank = jnp.sum(same.astype(jnp.float32), axis=0)
    slot = expert_ids * per + rank
    slot_line = jnp.arange(slots, dtype=jnp.float32)
    pack = slot_line[:, None] == slot[None, :]
    pack_grad = (pack & live[None, :]).astype(jnp.bfloat16)
    unpack = (slot[:, None] == slot_line[None, :]).astype(jnp.bfloat16)
    pack = pack.astype(jnp.bfloat16)
    spread = jnp.where(in_window, 1.0, 0.0) - gate_rows
    coef = (
        jnp.sum(
            jnp.where(
                route_rows[:, :, None] == columns.astype(jnp.float32)[None, None, :],
                spread[:, :, None],
                0.0,
            ),
            axis=0,
        )
        * weight[:, None]
    )
    weight_b = weight.astype(jnp.bfloat16).astype(jnp.float32)
    weight_col = jnp.broadcast_to(weight_b[:, None], (tok_count, LANES))[:, :1]

    vmem = pl.BlockSpec(memory_space=pltpu.VMEM)
    anywhere = pl.BlockSpec(memory_space=pl.ANY)
    bf16 = jnp.bfloat16
    return pl.pallas_call(
        functools.partial(layer_kernel, ep, tp, per),
        out_shape=(
            jax.ShapeDtypeStruct((tok_count, share), bf16),
            jax.ShapeDtypeStruct((tok_count, share), bf16),
            jax.ShapeDtypeStruct((tok_count, logits.shape[1]), jnp.float32),
        ),
        in_specs=[vmem] * 7 + [anywhere] * 3,
        out_specs=(vmem, vmem, vmem),
        scratch_shapes=[
            pltpu.VMEM((width, hidden_width), bf16),
            pltpu.VMEM((width, hidden_width), bf16),
            pltpu.VMEM((hidden_width, width), bf16),
            pltpu.VMEM((ep, per, share), bf16),
            pltpu.VMEM((ep, per, share), bf16),
            pltpu.VMEM((tp, slots, share), bf16),
            pltpu.VMEM((tp, slots, share), bf16),
            pltpu.VMEM((slots, hidden_width), jnp.float32),
            pltpu.VMEM((slots, hidden_width), jnp.float32),
            pltpu.VMEM((slots, hidden_width), bf16),
            pltpu.VMEM((tp, slots, share), bf16),
            pltpu.VMEM((tp - 1, slots, share), bf16),
            pltpu.VMEM((slots, share), bf16),
            pltpu.VMEM((slots, share), bf16),
            pltpu.VMEM((tp, slots, share + LANES), bf16),
            pltpu.VMEM((tp - 1, slots, share + LANES), bf16),
            pltpu.VMEM((slots, share + LANES), bf16),
            pltpu.VMEM((slots, share + LANES), bf16),
            pltpu.SemaphoreType.DMA((3,)),
            pltpu.SemaphoreType.DMA((4, ep)),
            pltpu.SemaphoreType.DMA((4, ep)),
            pltpu.SemaphoreType.DMA((4, ep * tp)),
            pltpu.SemaphoreType.DMA((4, ep * tp)),
        ],
        compiler_params=pltpu.CompilerParams(
            collective_id=0, has_side_effects=True, vmem_limit_bytes=56 * 1024 * 1024
        ),
        cost_estimate=pl.CostEstimate(
            flops=12 * slots * width * hidden_width,
            bytes_accessed=6 * width * hidden_width + 6 * tok_count * width,
            transcendentals=2 * slots * hidden_width,
        ),
        name="expert_layer",
    )(
        pack,
        pack_grad,
        unpack,
        weight_col,
        coef,
        tokens,
        out_grad,
        w_gate,
        w_up,
        w_down,
    )


def solution(mesh):
    in_specs = (
        P(("groups", "ep", "sp"), None),
        P(("groups", "ep", "sp"), None),
        P(("groups", "ep", "sp")),
        P(("groups", "ep", "sp"), None),
        P(("groups", "ep", "sp"), None),
        P(("groups", "ep", "sp")),
        P("ep", None, "tp"),
        P("ep", None, "tp"),
        P("ep", "tp", None),
    )
    out_specs = (
        P(("groups", "ep", "sp"), "tp"),
        P(("groups", "ep", "sp"), "tp"),
        P(("groups", "ep", "sp"), None),
    )
    return jax.shard_map(shards, mesh=mesh, in_specs=in_specs, out_specs=out_specs, check_vma=False)
```

```python
import functools

import jax
import jax.numpy as jnp
from jax import lax
from jax.experimental import pallas as pl
from jax.experimental.pallas import tpu as pltpu
from jax.sharding import PartitionSpec as P

MESH = pl.DeviceIdType.MESH
LANES = 128


def dot_nn(left, right):
    return jnp.dot(left, right, preferred_element_type=jnp.float32)


def dot_nt(left, right):
    return lax.dot_general(
        left, right, (((1,), (1,)), ((), ())), preferred_element_type=jnp.float32
    )


def layer_kernel(
    ep,
    tp,
    sp,
    per,
    logits_ref,
    routes_ref,
    owner_ref,
    length_ref,
    tokens_hbm,
    grads_hbm,
    gate_hbm,
    up_hbm,
    down_hbm,
    out_ref,
    token_grad_ref,
    router_ref,
    table,
    pack_ref,
    pack_grad_ref,
    unpack_ref,
    tokens_ref,
    grads_ref,
    w_gate,
    w_up,
    w_down,
    tok_send,
    grad_send,
    tok_near,
    grad_near,
    tok_all,
    grad_all,
    pre_gate,
    pre_up,
    hidden,
    out_part,
    out_recv,
    out_back,
    out_home,
    tg_part,
    tg_recv,
    tg_back,
    tg_home,
    w_sem,
    t_send,
    t_recv,
    z_send,
    z_recv,
    x_send,
    x_recv,
):
    share = tok_send.shape[2]
    tok_count = tokens_ref.shape[0]
    slots = ep * per
    top = routes_ref.shape[1]
    owner_count = ep * sp
    z = lax.axis_index("ep")
    x = lax.axis_index("tp")
    me = z * sp + lax.axis_index("sp")

    def rows_of(index):
        return pl.ds(pl.multiple_of(index * per, per), per)

    def peer(k):
        k = jnp.int32(k)
        both = 0
        bit = 1
        while bit < ep:
            both = both + bit * (lax.rem(lax.div(z, bit), 2) * lax.rem(lax.div(k, bit), 2))
            bit *= 2
        return z + k - 2 * both

    def owner_at(o):
        other = lax.rem(me + o, owner_count)
        return {"ep": lax.div(other, sp), "sp": lax.rem(other, sp)}

    barrier = pltpu.get_barrier_semaphore()

    @pl.loop(1, owner_count)
    def _(o):
        pl.semaphore_signal(barrier, inc=1, device_id=owner_at(o), device_id_type=MESH)

    for j in range(1, tp):
        pl.semaphore_signal(
            barrier, inc=1, device_id={"tp": lax.rem(x + j, tp)}, device_id_type=MESH
        )

    in_copies = [
        pltpu.make_async_copy(tokens_hbm, tokens_ref, w_sem.at[3]),
        pltpu.make_async_copy(grads_hbm, grads_ref, w_sem.at[4]),
    ]
    w_copies = [
        pltpu.make_async_copy(gate_hbm.at[0], w_gate, w_sem.at[0]),
        pltpu.make_async_copy(up_hbm.at[0], w_up, w_sem.at[1]),
        pltpu.make_async_copy(down_hbm.at[0], w_down, w_sem.at[2]),
    ]
    for copy in in_copies + w_copies:
        copy.start()

    square = (tok_count, tok_count)
    line = lax.broadcasted_iota(jnp.int32, square, 1)
    column = lax.broadcasted_iota(jnp.int32, square, 0)
    lanes = lax.broadcasted_iota(jnp.int32, logits_ref.shape, 1)
    logits = logits_ref[...]
    routes = routes_ref[...]
    picked = jnp.full(logits.shape, -1e30, jnp.float32)
    named = jnp.zeros(logits.shape, jnp.float32)
    for j in range(top):
        route = routes[:, j : j + 1]
        value = jnp.sum(jnp.where(lanes == route, logits, 0.0), axis=1, keepdims=True)
        picked = jnp.where(lanes == j, value, picked)
        named = jnp.where(lanes == top + j, route.astype(jnp.float32), named)
    raised = jnp.where(
        lanes < top, jnp.exp(picked - jnp.max(picked, axis=1, keepdims=True)), 0.0
    )
    merged = raised / jnp.sum(raised, axis=1, keepdims=True) + named
    table[me, 0 : 2 * top, :] = merged.T[0 : 2 * top, :]
    table[me, 2 * top : 3 * top, :] = jnp.broadcast_to(
        owner_ref[...].astype(jnp.float32), (top, tok_count)
    )

    def table_copy(o):
        return pltpu.make_async_remote_copy(
            src_ref=table.at[me],
            dst_ref=table.at[me],
            send_sem=t_send.at[o],
            recv_sem=t_recv.at[o],
            device_id=owner_at(o),
            device_id_type=MESH,
        )

    pl.semaphore_wait(barrier, owner_count - 1 + tp - 1)

    @pl.loop(1, owner_count)
    def _(o):
        table_copy(o).start()

    base = (me * tok_count).astype(jnp.float32)
    position = column.astype(jnp.float32) + base

    @pl.loop(1, owner_count)
    def _(o):
        table_copy(o).wait_recv()

    def gather(o, found):
        block = table[o]
        chosen = jnp.where(position == block[2 * top : 2 * top + 1, :], 1.0, 0.0)
        return found + lax.dot_general(
            chosen,
            block,
            (((1,), (1,)), ((), ())),
            precision=lax.Precision.HIGHEST,
            preferred_element_type=jnp.float32,
        )

    found = lax.fori_loop(
        0, owner_count, gather, jnp.zeros((tok_count, 3 * top), jnp.float32)
    )
    gate_rows = found[:, 0:top]
    route_rows = jnp.floor(found[:, top : 2 * top] + 0.5)
    inside = route_rows < ep
    expert = jnp.sum(jnp.where(inside, route_rows, 0.0), axis=1, keepdims=True)
    weight = jnp.sum(jnp.where(inside, gate_rows, 0.0), axis=1, keepdims=True)
    expert_square = jnp.broadcast_to(expert, square)
    same = (expert_square == expert_square.T) & (line < column)
    rank = jnp.sum(jnp.where(same, 1.0, 0.0), axis=1, keepdims=True)
    slot = expert * per + rank
    slot_line = jnp.broadcast_to(slot, square).T[0:1, :]
    slot_rows = lax.broadcasted_iota(jnp.int32, (slots, tok_count), 0).astype(jnp.float32)
    one_hot = jnp.where(slot_rows == slot_line, 1.0, 0.0)
    pack_ref[...] = one_hot.astype(jnp.bfloat16)
    live = line[0:1, :] < length_ref[...]
    pack_grad_ref[...] = jnp.where(live, one_hot, 0.0).astype(jnp.bfloat16)

    def slab(source_ref, placed, where, h):
        cols = pl.ds(pl.multiple_of(h * share, LANES), share)
        return dot_nn(placed[rows_of(where), :], source_ref[:, cols]).astype(jnp.bfloat16)

    def z_copy(kind, k):
        if kind < 2:
            sent, landed = ((tok_send, tok_all), (grad_send, grad_all))[kind]
            source, target = sent.at[k], landed.at[x, rows_of(z)]
        else:
            sent, landed = ((out_back, out_home), (tg_back, tg_home))[kind - 2]
            source, target = sent.at[rows_of(peer(k))], landed.at[rows_of(z)]
        return pltpu.make_async_remote_copy(
            src_ref=source,
            dst_ref=target,
            send_sem=z_send.at[kind, k],
            recv_sem=z_recv.at[kind, k],
            device_id={"ep": peer(k)},
            device_id_type=MESH,
        )

    def near_copy(kind):
        sent, landed = ((tok_near, tok_all), (grad_near, grad_all))[kind]
        return pltpu.make_async_remote_copy(
            src_ref=sent,
            dst_ref=landed.at[:, rows_of(z)],
            send_sem=z_send.at[kind, 1],
            recv_sem=z_recv.at[kind, 1],
            device_id={"ep": peer(1)},
            device_id_type=MESH,
        )

    def x_copy(kind, k, j):
        rows = rows_of(peer(k))
        target = lax.rem(x + j, tp)
        if kind < 2:
            buffer = (tok_all, grad_all)[kind]
            sent, landed = buffer.at[x, rows], buffer.at[x, rows]
        else:
            part, recv = ((out_part, out_recv), (tg_part, tg_recv))[kind - 2]
            sent, landed = part.at[target, rows], recv.at[j - 1, rows]
        return pltpu.make_async_remote_copy(
            src_ref=sent,
            dst_ref=landed,
            send_sem=x_send.at[kind, k * tp + j],
            recv_sem=x_recv.at[kind, k * tp + j],
            device_id={"tp": target},
            device_id_type=MESH,
        )

    def x_start(kind, k):
        for j in range(1, tp):
            x_copy(kind, k, j).start()

    def x_wait_recv(kind, k):
        for j in range(1, tp):
            x_copy(kind, k, j).wait_recv()

    in_copies[0].wait()

    @pl.loop(2, ep)
    def _(k):
        tok_send[k] = slab(tokens_ref, pack_ref, peer(k), x)
        z_copy(0, k).start()

    @pl.loop(0, tp)
    def _(h):
        tok_near[h] = slab(tokens_ref, pack_ref, peer(1), h)

    near_copy(0).start()

    @pl.loop(0, tp)
    def _(h):
        tok_all[h, rows_of(z), :] = slab(tokens_ref, pack_ref, z, h)

    in_copies[1].wait()

    @pl.loop(2, ep)
    def _(k):
        grad_send[k] = slab(grads_ref, pack_grad_ref, peer(k), x)

    @pl.loop(0, tp)
    def _(h):
        grad_near[h] = slab(grads_ref, pack_grad_ref, peer(1), h)
        grad_all[h, rows_of(z), :] = slab(grads_ref, pack_grad_ref, z, h)

    slot_columns = lax.broadcasted_iota(jnp.int32, (tok_count, slots), 1).astype(jnp.float32)
    unpack_ref[...] = jnp.where(slot_columns == slot, 1.0, 0.0).astype(jnp.bfloat16)
    coef = jnp.zeros(logits.shape, jnp.float32)
    spread = jnp.where(inside, 1.0, 0.0) - gate_rows
    lane_values = lanes.astype(jnp.float32)
    for j in range(top):
        coef = coef + jnp.where(
            lane_values == route_rows[:, j : j + 1], spread[:, j : j + 1], 0.0
        )
    router_ref[...] = coef * weight
    weight = weight.astype(jnp.bfloat16).astype(jnp.float32)

    def pump(kind, k):
        z_copy(kind, k).wait_recv()
        x_start(kind, k)
        if kind == 0:
            z_copy(1, k).start()

    def reduce_rows(kind, k):
        part, recv, back, home = (
            (out_part, out_recv, out_back, out_home),
            (tg_part, tg_recv, tg_back, tg_home),
        )[kind - 2]
        rows = rows_of(peer(k))
        x_wait_recv(kind, k)
        total = part[x, rows, :].astype(jnp.float32)
        for j in range(1, tp):
            total = total + recv[j - 1, rows, :].astype(jnp.float32)
        total = total.astype(jnp.bfloat16)

        @pl.when(k == 0)
        def _():
            home[rows, :] = total

        @pl.when(k > 0)
        def _():
            back[rows, :] = total
            z_copy(kind, k).start()

    for copy in w_copies:
        copy.wait()

    @pl.loop(0, ep)
    def _(k):
        rows = rows_of(peer(k))

        @pl.when((k >= 1) & (k + 1 < ep))
        def _():
            pump(0, k + 1)

        @pl.when(k == 1)
        def _():
            near_copy(0).wait_recv()
            near_copy(1).start()

        @pl.when(k >= 2)
        def _():
            x_wait_recv(0, k)

        gate = jnp.zeros((per, w_gate.shape[1]), jnp.float32)
        up = jnp.zeros((per, w_gate.shape[1]), jnp.float32)
        for h in range(tp):
            block = tok_all[h, rows, :]
            gate = gate + dot_nn(block, w_gate[h * share : (h + 1) * share, :])
            up = up + dot_nn(block, w_up[h * share : (h + 1) * share, :])
        pre_gate[rows, :] = gate
        pre_up[rows, :] = up
        hid = (gate * jax.nn.sigmoid(gate) * up).astype(jnp.bfloat16)
        hidden[rows, :] = hid
        for h in range(tp):
            out_part[h, rows, :] = dot_nn(
                hid, w_down[:, h * share : (h + 1) * share]
            ).astype(jnp.bfloat16)
        x_start(2, k)

    @pl.loop(0, ep)
    def _(k):
        rows = rows_of(peer(k))
        reduce_rows(2, lax.rem(k + 2, ep))

        @pl.when(k + 2 < ep)
        def _():
            pump(1, k + 2)

        @pl.when(k == 1)
        def _():
            near_copy(1).wait_recv()

        @pl.when(k >= 2)
        def _():
            x_wait_recv(1, k)

        back = jnp.zeros((per, w_gate.shape[1]), jnp.float32)
        for h in range(tp):
            back = back + dot_nt(grad_all[h, rows, :], w_down[:, h * share : (h + 1) * share])
        gate = pre_gate[rows, :]
        up = pre_up[rows, :]
        sig = jax.nn.sigmoid(gate)
        score = jnp.sum(hidden[rows, :].astype(jnp.float32) * back, axis=1, keepdims=True)
        score = jnp.broadcast_to(score, (per, LANES)).astype(jnp.bfloat16)
        grad_up = (back * (gate * sig)).astype(jnp.bfloat16)
        grad_gate = (back * up * (sig * (1.0 + gate * (1.0 - sig)))).astype(jnp.bfloat16)
        for h in range(tp):
            cols = slice(h * share, (h + 1) * share)
            tg_part[h, rows, 0:share] = (
                dot_nt(grad_gate, w_gate[cols, :]) + dot_nt(grad_up, w_up[cols, :])
            ).astype(jnp.bfloat16)
            tg_part[h, rows, share : share + LANES] = score
        x_start(3, k)

        @pl.when(k >= 1)
        def _():
            reduce_rows(3, k - 1)

    reduce_rows(3, jnp.int32(ep - 1))

    @pl.loop(1, ep)
    def _(k):
        z_copy(2, k).wait_recv()

    out_ref[...] = (dot_nn(unpack_ref[...], out_home[...]) * weight).astype(jnp.bfloat16)

    @pl.loop(1, ep)
    def _(k):
        z_copy(3, k).wait_recv()

    token_grad_ref[...] = (
        dot_nn(unpack_ref[...], tg_home[:, 0:share]) * weight
    ).astype(jnp.bfloat16)
    router_ref[...] = router_ref[...] * dot_nn(
        unpack_ref[...], tg_home[:, share : share + LANES]
    )

    @pl.loop(1, owner_count)
    def _(o):
        table_copy(o).wait_send()

    for kind in range(4):
        if kind < 2:
            near_copy(kind).wait_send()

        @pl.loop(2 if kind < 2 else 1, ep)
        def _(k):
            z_copy(kind, k).wait_send()

        @pl.loop(2 if kind < 2 else 0, ep)
        def _(k):
            for j in range(1, tp):
                x_copy(kind, k, j).wait_send()


def copy_kernel(a_in, b_in, c_in, a_out, b_out, c_out, sem):
    copies = [
        pltpu.make_async_copy(source, target, sem.at[i])
        for i, (source, target) in enumerate(((a_in, a_out), (b_in, b_out), (c_in, c_out)))
    ]
    for copy in copies:
        copy.start()
    for copy in copies:
        copy.wait()


def shards(logits, routes, owner, tokens, out_grad, resp_lengths, w_gate, w_up, w_down):
    tok_count, width = tokens.shape
    top = routes.shape[1]
    ep = lax.axis_size("ep")
    tp = lax.axis_size("tp")
    sp = lax.axis_size("sp")
    owner_count = ep * sp
    assert w_gate.shape[0] == 1 and ep >= 4 and ep & (ep - 1) == 0
    hidden_width = w_gate.shape[2]
    per = 2 * tok_count // ep
    slots = ep * per
    share = width // tp
    vmem = pl.BlockSpec(memory_space=pltpu.VMEM)
    anywhere = pl.BlockSpec(memory_space=pl.ANY)
    bf16 = jnp.bfloat16
    out_shape = (
        jax.ShapeDtypeStruct((tok_count, share), bf16),
        jax.ShapeDtypeStruct((tok_count, share), bf16),
        jax.ShapeDtypeStruct((tok_count, logits.shape[1]), jnp.float32),
    )
    results = pl.pallas_call(
        functools.partial(layer_kernel, ep, tp, sp, per),
        out_shape=out_shape,
        in_specs=[vmem] * 4 + [anywhere] * 5,
        out_specs=(vmem, vmem, vmem),
        scratch_shapes=[
            pltpu.VMEM((owner_count, 3 * top, tok_count), jnp.float32),
            pltpu.VMEM((slots, tok_count), bf16),
            pltpu.VMEM((slots, tok_count), bf16),
            pltpu.VMEM((tok_count, slots), bf16),
            pltpu.VMEM((tok_count, width), bf16),
            pltpu.VMEM((tok_count, width), bf16),
            pltpu.VMEM((width, hidden_width), bf16),
            pltpu.VMEM((width, hidden_width), bf16),
            pltpu.VMEM((hidden_width, width), bf16),
            pltpu.VMEM((ep, per, share), bf16),
            pltpu.VMEM((ep, per, share), bf16),
            pltpu.VMEM((tp, per, share), bf16),
            pltpu.VMEM((tp, per, share), bf16),
            pltpu.VMEM((tp, slots, share), bf16),
            pltpu.VMEM((tp, slots, share), bf16),
            pltpu.VMEM((slots, hidden_width), jnp.float32),
            pltpu.VMEM((slots, hidden_width), jnp.float32),
            pltpu.VMEM((slots, hidden_width), bf16),
            pltpu.VMEM((tp, slots, share), bf16),
            pltpu.VMEM((tp - 1, slots, share), bf16),
            pltpu.VMEM((slots, share), bf16),
            pltpu.VMEM((slots, share), bf16),
            pltpu.VMEM((tp, slots, share + LANES), bf16),
            pltpu.VMEM((tp - 1, slots, share + LANES), bf16),
            pltpu.VMEM((slots, share + LANES), bf16),
            pltpu.VMEM((slots, share + LANES), bf16),
            pltpu.SemaphoreType.DMA((5,)),
            pltpu.SemaphoreType.DMA((owner_count,)),
            pltpu.SemaphoreType.DMA((owner_count,)),
            pltpu.SemaphoreType.DMA((4, ep)),
            pltpu.SemaphoreType.DMA((4, ep)),
            pltpu.SemaphoreType.DMA((4, ep * tp)),
            pltpu.SemaphoreType.DMA((4, ep * tp)),
        ],
        compiler_params=pltpu.CompilerParams(
            collective_id=0, has_side_effects=True, vmem_limit_bytes=56 * 1024 * 1024
        ),
        cost_estimate=pl.CostEstimate(
            flops=12 * slots * width * hidden_width,
            bytes_accessed=6 * width * hidden_width + 6 * tok_count * width,
            transcendentals=2 * slots * hidden_width,
        ),
        name="expert_layer",
    )(
        logits,
        routes,
        owner.reshape(1, tok_count),
        resp_lengths.reshape(1, 1),
        tokens,
        out_grad,
        w_gate,
        w_up,
        w_down,
    )
    return pl.pallas_call(
        copy_kernel,
        out_shape=out_shape,
        in_specs=[anywhere] * 3,
        out_specs=(anywhere,) * 3,
        scratch_shapes=[pltpu.SemaphoreType.DMA((3,))],
        name="hand_over",
    )(*results)


def solution(mesh):
    in_specs = (
        P(("groups", "ep", "sp"), None),
        P(("groups", "ep", "sp"), None),
        P(("groups", "ep", "sp")),
        P(("groups", "ep", "sp"), None),
        P(("groups", "ep", "sp"), None),
        P(("groups", "ep", "sp")),
        P("ep", None, "tp"),
        P("ep", None, "tp"),
        P("ep", "tp", None),
    )
    out_specs = (
        P(("groups", "ep", "sp"), "tp"),
        P(("groups", "ep", "sp"), "tp"),
        P(("groups", "ep", "sp"), None),
    )
    return jax.shard_map(shards, mesh=mesh, in_specs=in_specs, out_specs=out_specs, check_vma=False)
```

```python
import functools

import jax
import jax.numpy as jnp
from jax import lax
from jax.experimental import pallas as pl
from jax.experimental.pallas import tpu as pltpu
from jax.sharding import PartitionSpec as P

MESH = pl.DeviceIdType.MESH
LANES = 128


def dot_nn(left, right):
    return jnp.dot(left, right, preferred_element_type=jnp.float32)


def dot_nt(left, right):
    return lax.dot_general(
        left, right, (((1,), (1,)), ((), ())), preferred_element_type=jnp.float32
    )


def layer_kernel(
    ep,
    tp,
    sp,
    per,
    logits_ref,
    routes_ref,
    owner_ref,
    length_ref,
    tokens_hbm,
    grads_hbm,
    gate_hbm,
    up_hbm,
    down_hbm,
    out_ref,
    token_grad_ref,
    router_ref,
    table,
    pack_ref,
    pack_grad_ref,
    unpack_ref,
    tokens_ref,
    grads_ref,
    w_gate,
    w_up,
    w_down,
    tok_send,
    grad_send,
    tok_near,
    grad_near,
    tok_all,
    grad_all,
    pre_gate,
    pre_up,
    hidden,
    out_part,
    out_recv,
    out_back,
    out_home,
    tg_part,
    tg_recv,
    tg_back,
    tg_home,
    w_sem,
    t_send,
    t_recv,
    z_send,
    z_recv,
    x_send,
    x_recv,
):
    share = tok_send.shape[2]
    tok_count = tokens_ref.shape[0]
    slots = ep * per
    top = routes_ref.shape[0]
    owner_count = ep * sp
    z = lax.axis_index("ep")
    x = lax.axis_index("tp")
    me = z * sp + lax.axis_index("sp")

    def rows_of(index):
        return pl.ds(pl.multiple_of(index * per, per), per)

    def peer(k):
        k = jnp.int32(k)
        both = 0
        bit = 1
        while bit < ep:
            both = both + bit * (lax.rem(lax.div(z, bit), 2) * lax.rem(lax.div(k, bit), 2))
            bit *= 2
        return z + k - 2 * both

    def owner_at(o):
        other = lax.rem(me + o, owner_count)
        return {"ep": lax.div(other, sp), "sp": lax.rem(other, sp)}

    barrier = pltpu.get_barrier_semaphore()

    @pl.loop(1, owner_count)
    def _(o):
        pl.semaphore_signal(barrier, inc=1, device_id=owner_at(o), device_id_type=MESH)

    for j in range(1, tp):
        pl.semaphore_signal(
            barrier, inc=1, device_id={"tp": lax.rem(x + j, tp)}, device_id_type=MESH
        )

    in_copies = [
        pltpu.make_async_copy(tokens_hbm, tokens_ref, w_sem.at[3]),
        pltpu.make_async_copy(grads_hbm, grads_ref, w_sem.at[4]),
    ]
    w_copies = [
        pltpu.make_async_copy(gate_hbm.at[0], w_gate, w_sem.at[0]),
        pltpu.make_async_copy(up_hbm.at[0], w_up, w_sem.at[1]),
        pltpu.make_async_copy(down_hbm.at[0], w_down, w_sem.at[2]),
    ]
    for copy in in_copies + w_copies:
        copy.start()

    square = (tok_count, tok_count)
    line = lax.broadcasted_iota(jnp.int32, square, 1)
    column = lax.broadcasted_iota(jnp.int32, square, 0)
    lanes = lax.broadcasted_iota(jnp.int32, logits_ref.shape, 1)
    logits_t = logits_ref[...].T
    routes_t = routes_ref[...]
    expert_line = lax.broadcasted_iota(jnp.int32, logits_t.shape, 0)
    picked = jnp.concatenate(
        [
            jnp.sum(
                jnp.where(expert_line == routes_t[i : i + 1, :], logits_t, 0.0),
                axis=0,
                keepdims=True,
            )
            for i in range(top)
        ],
        axis=0,
    )
    raised = jnp.exp(picked - jnp.max(picked, axis=0, keepdims=True))
    table[me, 0:top, :] = raised / jnp.sum(raised, axis=0, keepdims=True)
    table[me, top : 2 * top, :] = routes_t.astype(jnp.float32)
    held = jnp.sum(jnp.where(routes_t < ep, routes_t, 0), axis=0, keepdims=True)
    place = lax.broadcasted_iota(jnp.int32, (top, tok_count), 0)
    table[me, 2 * top : 3 * top, :] = jnp.where(
        place == 0, owner_ref[...], jnp.where(place == 1, held, 0)
    ).astype(jnp.float32)

    def table_copy(o):
        return pltpu.make_async_remote_copy(
            src_ref=table.at[me],
            dst_ref=table.at[me],
            send_sem=t_send.at[o],
            recv_sem=t_recv.at[o],
            device_id=owner_at(o),
            device_id_type=MESH,
        )

    pl.semaphore_wait(barrier, owner_count - 1 + tp - 1)

    @pl.loop(1, owner_count)
    def _(o):
        table_copy(o).start()

    base = (me * tok_count).astype(jnp.float32)
    position = column.astype(jnp.float32) + base

    @pl.loop(1, owner_count)
    def _(o):
        table_copy(o).wait_recv()

    def find(o, found):
        block = table[o]
        return found + jnp.where(
            position == block[2 * top : 2 * top + 1, :],
            block[2 * top + 1 : 2 * top + 2, :],
            0.0,
        )

    expert = jnp.sum(
        lax.fori_loop(0, owner_count, find, jnp.zeros(square, jnp.float32)),
        axis=1,
        keepdims=True,
    )
    expert_square = jnp.broadcast_to(expert, square)
    expert_row = expert_square.T[0:1, :]
    slot_line = expert_row * per + jnp.sum(
        jnp.where((expert_square == expert_row) & (column < line), 1.0, 0.0),
        axis=0,
        keepdims=True,
    )
    slot_rows = lax.broadcasted_iota(jnp.int32, (slots, tok_count), 0).astype(jnp.float32)
    one_hot = jnp.where(slot_rows == slot_line, 1.0, 0.0)
    pack_ref[...] = one_hot.astype(jnp.bfloat16)
    live = line[0:1, :] < length_ref[...]
    pack_grad_ref[...] = jnp.where(live, one_hot, 0.0).astype(jnp.bfloat16)

    def slab(source_ref, placed, where, h):
        cols = pl.ds(pl.multiple_of(h * share, LANES), share)
        return dot_nn(placed[rows_of(where), :], source_ref[:, cols]).astype(jnp.bfloat16)

    def z_copy(kind, k):
        if kind < 2:
            sent, landed = ((tok_send, tok_all), (grad_send, grad_all))[kind]
            source, target = sent.at[k], landed.at[x, rows_of(z)]
        else:
            sent, landed = ((out_back, out_home), (tg_back, tg_home))[kind - 2]
            source, target = sent.at[rows_of(peer(k))], landed.at[rows_of(z)]
        return pltpu.make_async_remote_copy(
            src_ref=source,
            dst_ref=target,
            send_sem=z_send.at[kind, k],
            recv_sem=z_recv.at[kind, k],
            device_id={"ep": peer(k)},
            device_id_type=MESH,
        )

    def near_copy(kind):
        sent, landed = ((tok_near, tok_all), (grad_near, grad_all))[kind]
        return pltpu.make_async_remote_copy(
            src_ref=sent,
            dst_ref=landed.at[:, rows_of(z)],
            send_sem=z_send.at[kind, 1],
            recv_sem=z_recv.at[kind, 1],
            device_id={"ep": peer(1)},
            device_id_type=MESH,
        )

    def x_copy(kind, k, j):
        rows = rows_of(peer(k))
        target = lax.rem(x + j, tp)
        if kind < 2:
            buffer = (tok_all, grad_all)[kind]
            sent, landed = buffer.at[x, rows], buffer.at[x, rows]
        else:
            part, recv = ((out_part, out_recv), (tg_part, tg_recv))[kind - 2]
            sent, landed = part.at[target, rows], recv.at[j - 1, rows]
        return pltpu.make_async_remote_copy(
            src_ref=sent,
            dst_ref=landed,
            send_sem=x_send.at[kind, k * tp + j],
            recv_sem=x_recv.at[kind, k * tp + j],
            device_id={"tp": target},
            device_id_type=MESH,
        )

    def x_start(kind, k):
        for j in range(1, tp):
            x_copy(kind, k, j).start()

    def x_wait_recv(kind, k):
        for j in range(1, tp):
            x_copy(kind, k, j).wait_recv()

    in_copies[0].wait()

    @pl.loop(2, ep)
    def _(k):
        tok_send[k] = slab(tokens_ref, pack_ref, peer(k), x)
        z_copy(0, k).start()

    @pl.loop(0, tp)
    def _(h):
        tok_near[h] = slab(tokens_ref, pack_ref, peer(1), h)

    near_copy(0).start()

    @pl.loop(0, tp)
    def _(h):
        tok_all[h, rows_of(z), :] = slab(tokens_ref, pack_ref, z, h)

    in_copies[1].wait()

    @pl.loop(2, ep)
    def _(k):
        grad_send[k] = slab(grads_ref, pack_grad_ref, peer(k), x)

    z_copy(1, 2).start()

    @pl.loop(0, tp)
    def _(h):
        grad_near[h] = slab(grads_ref, pack_grad_ref, peer(1), h)
        grad_all[h, rows_of(z), :] = slab(grads_ref, pack_grad_ref, z, h)

    def gather(o, found):
        block = table[o]
        chosen = jnp.where(position == block[2 * top : 2 * top + 1, :], 1.0, 0.0)
        return found + lax.dot_general(
            chosen,
            block,
            (((1,), (1,)), ((), ())),
            precision=lax.Precision.HIGHEST,
            preferred_element_type=jnp.float32,
        )

    found = lax.fori_loop(
        0, owner_count, gather, jnp.zeros((tok_count, 3 * top), jnp.float32)
    )
    gate_rows = found[:, 0:top]
    route_rows = found[:, top : 2 * top]
    inside = route_rows < ep
    weight = jnp.sum(jnp.where(inside, gate_rows, 0.0), axis=1, keepdims=True)
    slot = expert * per + jnp.sum(
        jnp.where((expert_square == expert_row) & (line < column), 1.0, 0.0),
        axis=1,
        keepdims=True,
    )
    lanes = lax.broadcasted_iota(jnp.int32, logits_ref.shape, 1)
    slot_columns = lax.broadcasted_iota(jnp.int32, (tok_count, slots), 1).astype(jnp.float32)
    unpack_ref[...] = jnp.where(slot_columns == slot, 1.0, 0.0).astype(jnp.bfloat16)
    coef = jnp.zeros(logits_ref.shape, jnp.float32)
    spread = jnp.where(inside, 1.0, 0.0) - gate_rows
    lane_values = lanes.astype(jnp.float32)
    for j in range(top):
        coef = coef + jnp.where(
            lane_values == route_rows[:, j : j + 1], spread[:, j : j + 1], 0.0
        )
    router_ref[...] = coef * weight
    weight = weight.astype(jnp.bfloat16).astype(jnp.float32)

    def pump(kind, k):
        z_copy(kind, k).wait_recv()
        x_start(kind, k)
        if kind == 0:

            @pl.when(k + 1 < ep)
            def _():
                z_copy(1, k + 1).start()

    def reduce_rows(kind, k):
        part, recv, back, home = (
            (out_part, out_recv, out_back, out_home),
            (tg_part, tg_recv, tg_back, tg_home),
        )[kind - 2]
        rows = rows_of(peer(k))
        x_wait_recv(kind, k)
        total = part[x, rows, :].astype(jnp.float32)
        for j in range(1, tp):
            total = total + recv[j - 1, rows, :].astype(jnp.float32)
        total = total.astype(jnp.bfloat16)

        @pl.when(k == 0)
        def _():
            home[rows, :] = total

        @pl.when(k > 0)
        def _():
            back[rows, :] = total
            z_copy(kind, k).start()

    for copy in w_copies:
        copy.wait()

    @pl.loop(0, ep)
    def _(k):
        rows = rows_of(peer(k))

        @pl.when((k >= 1) & (k + 1 < ep))
        def _():
            pump(0, k + 1)

        @pl.when(k == 1)
        def _():
            near_copy(0).wait_recv()
            near_copy(1).start()

        @pl.when(k >= 2)
        def _():
            x_wait_recv(0, k)

        gate = jnp.zeros((per, w_gate.shape[1]), jnp.float32)
        up = jnp.zeros((per, w_gate.shape[1]), jnp.float32)
        for h in range(tp):
            block = tok_all[h, rows, :]
            gate = gate + dot_nn(block, w_gate[h * share : (h + 1) * share, :])
            up = up + dot_nn(block, w_up[h * share : (h + 1) * share, :])
        pre_gate[rows, :] = gate
        pre_up[rows, :] = up
        hid = (gate * jax.nn.sigmoid(gate) * up).astype(jnp.bfloat16)
        hidden[rows, :] = hid
        for h in range(tp):
            out_part[h, rows, :] = dot_nn(
                hid, w_down[:, h * share : (h + 1) * share]
            ).astype(jnp.bfloat16)

        @pl.when(k != 1)
        def _():
            x_start(2, k)

    x_start(2, jnp.int32(1))

    @pl.loop(0, ep)
    def _(k):
        rows = rows_of(peer(k))
        reduce_rows(2, lax.select(k + 2 < ep, k + 2, ep - 1 - k))

        @pl.when(k + 2 < ep)
        def _():
            pump(1, k + 2)

        @pl.when(k == 1)
        def _():
            near_copy(1).wait_recv()

        @pl.when(k >= 2)
        def _():
            x_wait_recv(1, k)

        back = jnp.zeros((per, w_gate.shape[1]), jnp.float32)
        for h in range(tp):
            back = back + dot_nt(grad_all[h, rows, :], w_down[:, h * share : (h + 1) * share])
        gate = pre_gate[rows, :]
        up = pre_up[rows, :]
        sig = jax.nn.sigmoid(gate)
        score = jnp.sum(hidden[rows, :].astype(jnp.float32) * back, axis=1, keepdims=True)
        score = jnp.broadcast_to(score, (per, LANES)).astype(jnp.bfloat16)
        grad_up = (back * (gate * sig)).astype(jnp.bfloat16)
        grad_gate = (back * up * (sig * (1.0 + gate * (1.0 - sig)))).astype(jnp.bfloat16)
        for h in range(tp):
            cols = slice(h * share, (h + 1) * share)
            tg_part[h, rows, 0:share] = (
                dot_nt(grad_gate, w_gate[cols, :]) + dot_nt(grad_up, w_up[cols, :])
            ).astype(jnp.bfloat16)
            tg_part[h, rows, share : share + LANES] = score

        @pl.when(k >= 2)
        def _():
            x_start(3, k)

        @pl.when(k >= 3)
        def _():
            reduce_rows(3, k - 1)

    x_start(3, jnp.int32(1))
    x_start(3, jnp.int32(0))
    reduce_rows(3, jnp.int32(ep - 1))
    reduce_rows(3, jnp.int32(1))
    reduce_rows(3, jnp.int32(0))

    @pl.loop(1, ep)
    def _(k):
        z_copy(2, k).wait_recv()

    out_ref[...] = (dot_nn(unpack_ref[...], out_home[...]) * weight).astype(jnp.bfloat16)

    @pl.loop(1, ep)
    def _(k):
        z_copy(3, k).wait_recv()

    token_grad_ref[...] = (
        dot_nn(unpack_ref[...], tg_home[:, 0:share]) * weight
    ).astype(jnp.bfloat16)
    router_ref[...] = router_ref[...] * dot_nn(
        unpack_ref[...], tg_home[:, share : share + LANES]
    )

    @pl.loop(1, owner_count)
    def _(o):
        table_copy(o).wait_send()

    for kind in range(4):
        if kind < 2:
            near_copy(kind).wait_send()

        @pl.loop(2 if kind < 2 else 1, ep)
        def _(k):
            z_copy(kind, k).wait_send()

        @pl.loop(2 if kind < 2 else 0, ep)
        def _(k):
            for j in range(1, tp):
                x_copy(kind, k, j).wait_send()


def copy_kernel(a_in, b_in, c_in, a_out, b_out, c_out):
    a_out[...] = a_in[...]
    b_out[...] = b_in[...]
    c_out[...] = c_in[...]


def shards(logits, routes, owner, tokens, out_grad, resp_lengths, w_gate, w_up, w_down):
    tok_count, width = tokens.shape
    top = routes.shape[1]
    ep = lax.axis_size("ep")
    tp = lax.axis_size("tp")
    sp = lax.axis_size("sp")
    owner_count = ep * sp
    assert w_gate.shape[0] == 1 and ep >= 4 and ep & (ep - 1) == 0
    hidden_width = w_gate.shape[2]
    per = 2 * tok_count // ep
    slots = ep * per
    share = width // tp
    vmem = pl.BlockSpec(memory_space=pltpu.VMEM)
    anywhere = pl.BlockSpec(memory_space=pl.ANY)
    bf16 = jnp.bfloat16
    out_shape = (
        jax.ShapeDtypeStruct((tok_count, share), bf16),
        jax.ShapeDtypeStruct((tok_count, share), bf16),
        jax.ShapeDtypeStruct((tok_count, logits.shape[1]), jnp.float32),
    )
    results = pl.pallas_call(
        functools.partial(layer_kernel, ep, tp, sp, per),
        out_shape=out_shape,
        in_specs=[vmem] * 4 + [anywhere] * 5,
        out_specs=(vmem, vmem, vmem),
        scratch_shapes=[
            pltpu.VMEM((owner_count, 3 * top, tok_count), jnp.float32),
            pltpu.VMEM((slots, tok_count), bf16),
            pltpu.VMEM((slots, tok_count), bf16),
            pltpu.VMEM((tok_count, slots), bf16),
            pltpu.VMEM((tok_count, width), bf16),
            pltpu.VMEM((tok_count, width), bf16),
            pltpu.VMEM((width, hidden_width), bf16),
            pltpu.VMEM((width, hidden_width), bf16),
            pltpu.VMEM((hidden_width, width), bf16),
            pltpu.VMEM((ep, per, share), bf16),
            pltpu.VMEM((ep, per, share), bf16),
            pltpu.VMEM((tp, per, share), bf16),
            pltpu.VMEM((tp, per, share), bf16),
            pltpu.VMEM((tp, slots, share), bf16),
            pltpu.VMEM((tp, slots, share), bf16),
            pltpu.VMEM((slots, hidden_width), jnp.float32),
            pltpu.VMEM((slots, hidden_width), jnp.float32),
            pltpu.VMEM((slots, hidden_width), bf16),
            pltpu.VMEM((tp, slots, share), bf16),
            pltpu.VMEM((tp - 1, slots, share), bf16),
            pltpu.VMEM((slots, share), bf16),
            pltpu.VMEM((slots, share), bf16),
            pltpu.VMEM((tp, slots, share + LANES), bf16),
            pltpu.VMEM((tp - 1, slots, share + LANES), bf16),
            pltpu.VMEM((slots, share + LANES), bf16),
            pltpu.VMEM((slots, share + LANES), bf16),
            pltpu.SemaphoreType.DMA((5,)),
            pltpu.SemaphoreType.DMA((owner_count,)),
            pltpu.SemaphoreType.DMA((owner_count,)),
            pltpu.SemaphoreType.DMA((4, ep)),
            pltpu.SemaphoreType.DMA((4, ep)),
            pltpu.SemaphoreType.DMA((4, ep * tp)),
            pltpu.SemaphoreType.DMA((4, ep * tp)),
        ],
        compiler_params=pltpu.CompilerParams(
            collective_id=0, has_side_effects=True, vmem_limit_bytes=56 * 1024 * 1024
        ),
        cost_estimate=pl.CostEstimate(
            flops=12 * slots * width * hidden_width,
            bytes_accessed=6 * width * hidden_width + 6 * tok_count * width,
            transcendentals=2 * slots * hidden_width,
        ),
        name="expert_layer",
    )(
        logits,
        routes.T,
        owner.reshape(1, tok_count),
        resp_lengths.reshape(1, 1),
        tokens,
        out_grad,
        w_gate,
        w_up,
        w_down,
    )
    return pl.pallas_call(
        copy_kernel,
        out_shape=out_shape,
        in_specs=[vmem] * 3,
        out_specs=(vmem,) * 3,
        name="hand_over",
    )(*results)


def solution(mesh):
    in_specs = (
        P(("groups", "ep", "sp"), None),
        P(("groups", "ep", "sp"), None),
        P(("groups", "ep", "sp")),
        P(("groups", "ep", "sp"), None),
        P(("groups", "ep", "sp"), None),
        P(("groups", "ep", "sp")),
        P("ep", None, "tp"),
        P("ep", None, "tp"),
        P("ep", "tp", None),
    )
    out_specs = (
        P(("groups", "ep", "sp"), "tp"),
        P(("groups", "ep", "sp"), "tp"),
        P(("groups", "ep", "sp"), None),
    )
    return jax.shard_map(shards, mesh=mesh, in_specs=in_specs, out_specs=out_specs, check_vma=False)
```

```python
import functools

import jax
import jax.numpy as jnp
from jax import lax
from jax.experimental import pallas as pl
from jax.experimental.pallas import tpu as pltpu
from jax.sharding import PartitionSpec as P

MESH = pl.DeviceIdType.MESH
LANES = 128


def dot_nn(left, right):
    return jnp.dot(left, right, preferred_element_type=jnp.float32)


def dot_nt(left, right):
    return lax.dot_general(
        left, right, (((1,), (1,)), ((), ())), preferred_element_type=jnp.float32
    )


def layer_kernel(
    ep,
    tp,
    sp,
    per,
    logits_ref,
    routes_ref,
    owner_ref,
    length_ref,
    tokens_hbm,
    grads_hbm,
    gate_hbm,
    up_hbm,
    down_hbm,
    out_ref,
    token_grad_ref,
    router_ref,
    table,
    pack_ref,
    pack_grad_ref,
    unpack_ref,
    tokens_ref,
    grads_ref,
    w_gate,
    w_up,
    w_down,
    tok_send,
    grad_send,
    tok_near,
    grad_near,
    tok_all,
    grad_all,
    pre_gate,
    pre_up,
    hidden,
    out_part,
    out_recv,
    out_back,
    out_home,
    tg_part,
    tg_recv,
    tg_back,
    tg_home,
    w_sem,
    t_send,
    t_recv,
    z_send,
    z_recv,
    x_send,
    x_recv,
):
    share = tok_send.shape[2]
    tok_count = tokens_ref.shape[0]
    slots = ep * per
    top = routes_ref.shape[0]
    owner_count = ep * sp
    z = lax.axis_index("ep")
    x = lax.axis_index("tp")
    me = z * sp + lax.axis_index("sp")

    def rows_of(index):
        return pl.ds(pl.multiple_of(index * per, per), per)

    def peer(k):
        k = jnp.int32(k)
        both = 0
        bit = 1
        while bit < ep:
            both = both + bit * (lax.rem(lax.div(z, bit), 2) * lax.rem(lax.div(k, bit), 2))
            bit *= 2
        return z + k - 2 * both

    def owner_at(o):
        other = lax.rem(me + o, owner_count)
        return {"ep": lax.div(other, sp), "sp": lax.rem(other, sp)}

    barrier = pltpu.get_barrier_semaphore()

    @pl.loop(1, owner_count)
    def _(o):
        pl.semaphore_signal(barrier, inc=1, device_id=owner_at(o), device_id_type=MESH)

    for j in range(1, tp):
        pl.semaphore_signal(
            barrier, inc=1, device_id={"tp": lax.rem(x + j, tp)}, device_id_type=MESH
        )

    in_copies = [
        pltpu.make_async_copy(tokens_hbm, tokens_ref, w_sem.at[3]),
        pltpu.make_async_copy(grads_hbm, grads_ref, w_sem.at[4]),
    ]
    w_copies = [
        pltpu.make_async_copy(gate_hbm.at[0], w_gate, w_sem.at[0]),
        pltpu.make_async_copy(up_hbm.at[0], w_up, w_sem.at[1]),
        pltpu.make_async_copy(down_hbm.at[0], w_down, w_sem.at[2]),
    ]
    for copy in in_copies + w_copies:
        copy.start()

    square = (tok_count, tok_count)
    line = lax.broadcasted_iota(jnp.int32, square, 1)
    column = lax.broadcasted_iota(jnp.int32, square, 0)
    lanes = lax.broadcasted_iota(jnp.int32, logits_ref.shape, 1)
    logits_t = logits_ref[...].T
    routes_t = routes_ref[...]
    expert_line = lax.broadcasted_iota(jnp.int32, logits_t.shape, 0)
    picked = jnp.concatenate(
        [
            jnp.sum(
                jnp.where(expert_line == routes_t[i : i + 1, :], logits_t, 0.0),
                axis=0,
                keepdims=True,
            )
            for i in range(top)
        ],
        axis=0,
    )
    raised = jnp.exp(picked - jnp.max(picked, axis=0, keepdims=True))
    table[me, 0:top, :] = raised / jnp.sum(raised, axis=0, keepdims=True)
    table[me, top : 2 * top, :] = routes_t.astype(jnp.float32)
    held = jnp.sum(jnp.where(routes_t < ep, routes_t, 0), axis=0, keepdims=True)
    place = lax.broadcasted_iota(jnp.int32, (top, tok_count), 0)
    table[me, 2 * top : 3 * top, :] = jnp.where(
        place == 0, owner_ref[...], jnp.where(place == 1, held, 0)
    ).astype(jnp.float32)

    def table_copy(o):
        return pltpu.make_async_remote_copy(
            src_ref=table.at[me],
            dst_ref=table.at[me],
            send_sem=t_send.at[o],
            recv_sem=t_recv.at[o],
            device_id=owner_at(o),
            device_id_type=MESH,
        )

    pl.semaphore_wait(barrier, owner_count - 1 + tp - 1)

    @pl.loop(1, owner_count)
    def _(o):
        table_copy(o).start()

    base = (me * tok_count).astype(jnp.float32)
    position = column.astype(jnp.float32) + base

    @pl.loop(1, owner_count)
    def _(o):
        table_copy(o).wait_recv()

    def find(o, found):
        block = table[o]
        return found + jnp.where(
            position == block[2 * top : 2 * top + 1, :],
            block[2 * top + 1 : 2 * top + 2, :],
            0.0,
        )

    expert = jnp.sum(
        lax.fori_loop(0, owner_count, find, jnp.zeros(square, jnp.float32)),
        axis=1,
        keepdims=True,
    )
    expert_square = jnp.broadcast_to(expert, square)
    expert_row = expert_square.T[0:1, :]
    slot_line = expert_row * per + jnp.sum(
        jnp.where((expert_square == expert_row) & (column < line), 1.0, 0.0),
        axis=0,
        keepdims=True,
    )
    slot_rows = lax.broadcasted_iota(jnp.int32, (slots, tok_count), 0).astype(jnp.float32)
    one_hot = jnp.where(slot_rows == slot_line, 1.0, 0.0)
    pack_ref[...] = one_hot.astype(jnp.bfloat16)
    live = line[0:1, :] < length_ref[...]
    pack_grad_ref[...] = jnp.where(live, one_hot, 0.0).astype(jnp.bfloat16)

    def slab(source_ref, placed, where, h):
        cols = pl.ds(pl.multiple_of(h * share, LANES), share)
        return dot_nn(placed[rows_of(where), :], source_ref[:, cols]).astype(jnp.bfloat16)

    def z_copy(kind, k):
        if kind < 2:
            sent, landed = ((tok_send, tok_all), (grad_send, grad_all))[kind]
            source, target = sent.at[k], landed.at[x, rows_of(z)]
        else:
            sent, landed = ((out_back, out_home), (tg_back, tg_home))[kind - 2]
            source, target = sent.at[rows_of(peer(k))], landed.at[rows_of(z)]
        return pltpu.make_async_remote_copy(
            src_ref=source,
            dst_ref=target,
            send_sem=z_send.at[kind, k],
            recv_sem=z_recv.at[kind, k],
            device_id={"ep": peer(k)},
            device_id_type=MESH,
        )

    def near_copy(kind):
        sent, landed = ((tok_near, tok_all), (grad_near, grad_all))[kind]
        return pltpu.make_async_remote_copy(
            src_ref=sent,
            dst_ref=landed.at[:, rows_of(z)],
            send_sem=z_send.at[kind, 1],
            recv_sem=z_recv.at[kind, 1],
            device_id={"ep": peer(1)},
            device_id_type=MESH,
        )

    def x_copy(kind, k, j):
        rows = rows_of(peer(k))
        target = lax.rem(x + j, tp)
        if kind < 2:
            buffer = (tok_all, grad_all)[kind]
            sent, landed = buffer.at[x, rows], buffer.at[x, rows]
        else:
            part, recv = ((out_part, out_recv), (tg_part, tg_recv))[kind - 2]
            sent, landed = part.at[target, rows], recv.at[j - 1, rows]
        return pltpu.make_async_remote_copy(
            src_ref=sent,
            dst_ref=landed,
            send_sem=x_send.at[kind, k * tp + j],
            recv_sem=x_recv.at[kind, k * tp + j],
            device_id={"tp": target},
            device_id_type=MESH,
        )

    def x_start(kind, k):
        for j in range(1, tp):
            x_copy(kind, k, j).start()

    def x_wait_recv(kind, k):
        for j in range(1, tp):
            x_copy(kind, k, j).wait_recv()

    in_copies[0].wait()

    @pl.loop(2, ep)
    def _(k):
        tok_send[k] = slab(tokens_ref, pack_ref, peer(k), x)
        z_copy(0, k).start()

    @pl.loop(0, tp)
    def _(h):
        tok_near[h] = slab(tokens_ref, pack_ref, peer(1), h)

    near_copy(0).start()

    @pl.loop(0, tp)
    def _(h):
        tok_all[h, rows_of(z), :] = slab(tokens_ref, pack_ref, z, h)

    in_copies[1].wait()

    @pl.loop(2, ep)
    def _(k):
        grad_send[k] = slab(grads_ref, pack_grad_ref, peer(k), x)

    z_copy(1, 2).start()

    @pl.loop(0, tp)
    def _(h):
        grad_near[h] = slab(grads_ref, pack_grad_ref, peer(1), h)
        grad_all[h, rows_of(z), :] = slab(grads_ref, pack_grad_ref, z, h)

    def gather(o, found):
        block = table[o]
        chosen = jnp.where(position == block[2 * top : 2 * top + 1, :], 1.0, 0.0)
        return found + lax.dot_general(
            chosen,
            block,
            (((1,), (1,)), ((), ())),
            precision=lax.Precision.HIGHEST,
            preferred_element_type=jnp.float32,
        )

    found = lax.fori_loop(
        0, owner_count, gather, jnp.zeros((tok_count, 3 * top), jnp.float32)
    )
    gate_rows = found[:, 0:top]
    route_rows = found[:, top : 2 * top]
    inside = route_rows < ep
    weight = jnp.sum(jnp.where(inside, gate_rows, 0.0), axis=1, keepdims=True)
    slot = expert * per + jnp.sum(
        jnp.where((expert_square == expert_row) & (line < column), 1.0, 0.0),
        axis=1,
        keepdims=True,
    )
    lanes = lax.broadcasted_iota(jnp.int32, logits_ref.shape, 1)
    slot_columns = lax.broadcasted_iota(jnp.int32, (tok_count, slots), 1).astype(jnp.float32)
    unpack_ref[...] = jnp.where(slot_columns == slot, 1.0, 0.0).astype(jnp.bfloat16)
    coef = jnp.zeros(logits_ref.shape, jnp.float32)
    spread = jnp.where(inside, 1.0, 0.0) - gate_rows
    lane_values = lanes.astype(jnp.float32)
    for j in range(top):
        coef = coef + jnp.where(
            lane_values == route_rows[:, j : j + 1], spread[:, j : j + 1], 0.0
        )
    router_ref[...] = coef * weight
    weight = weight.astype(jnp.bfloat16).astype(jnp.float32)

    def pump(kind, k):
        z_copy(kind, k).wait_recv()
        x_start(kind, k)
        if kind == 0:

            @pl.when(k + 1 < ep)
            def _():
                z_copy(1, k + 1).start()

    def reduce_rows(kind, k):
        part, recv, back, home = (
            (out_part, out_recv, out_back, out_home),
            (tg_part, tg_recv, tg_back, tg_home),
        )[kind - 2]
        rows = rows_of(peer(k))
        x_wait_recv(kind, k)
        total = part[x, rows, :].astype(jnp.float32)
        for j in range(1, tp):
            total = total + recv[j - 1, rows, :].astype(jnp.float32)
        total = total.astype(jnp.bfloat16)

        @pl.when(k == 0)
        def _():
            home[rows, :] = total

        @pl.when(k > 0)
        def _():
            back[rows, :] = total
            z_copy(kind, k).start()

    for copy in w_copies:
        copy.wait()

    @pl.loop(0, ep)
    def _(k):
        rows = rows_of(peer(k))

        @pl.when((k >= 1) & (k + 1 < ep))
        def _():
            pump(0, k + 1)

        @pl.when(k == 1)
        def _():
            near_copy(0).wait_recv()
            near_copy(1).start()

        @pl.when(k >= 2)
        def _():
            x_wait_recv(0, k)

        gate = jnp.zeros((per, w_gate.shape[1]), jnp.float32)
        up = jnp.zeros((per, w_gate.shape[1]), jnp.float32)
        for h in range(tp):
            block = tok_all[h, rows, :]
            gate = gate + dot_nn(block, w_gate[h * share : (h + 1) * share, :])
            up = up + dot_nn(block, w_up[h * share : (h + 1) * share, :])
        pre_gate[rows, :] = gate
        pre_up[rows, :] = up
        hid = (gate * jax.nn.sigmoid(gate) * up).astype(jnp.bfloat16)
        hidden[rows, :] = hid
        for h in range(tp):
            out_part[h, rows, :] = dot_nn(
                hid, w_down[:, h * share : (h + 1) * share]
            ).astype(jnp.bfloat16)

        @pl.when(k != 1)
        def _():
            x_start(2, k)

    x_start(2, jnp.int32(1))

    @pl.loop(0, ep)
    def _(p):
        k = lax.select(p == 0, 0, lax.select(p + 1 < ep, p + 1, 1))
        rows = rows_of(peer(k))

        @pl.when(k >= 3)
        def _():
            pump(1, k)

        reduce_rows(2, lax.select(p + 2 < ep, p + 2, ep - 1 - p))

        @pl.when(p == 0)
        def _():
            pump(1, 2)

        @pl.when(k >= 3)
        def _():
            reduce_rows(3, k - 1)

        @pl.when(k == 1)
        def _():
            near_copy(1).wait_recv()

        @pl.when(k >= 2)
        def _():
            x_wait_recv(1, k)

        back = jnp.zeros((per, w_gate.shape[1]), jnp.float32)
        for h in range(tp):
            back = back + dot_nt(grad_all[h, rows, :], w_down[:, h * share : (h + 1) * share])
        gate = pre_gate[rows, :]
        up = pre_up[rows, :]
        sig = jax.nn.sigmoid(gate)
        score = jnp.sum(hidden[rows, :].astype(jnp.float32) * back, axis=1, keepdims=True)
        score = jnp.broadcast_to(score, (per, LANES)).astype(jnp.bfloat16)
        grad_up = (back * (gate * sig)).astype(jnp.bfloat16)
        grad_gate = (back * up * (sig * (1.0 + gate * (1.0 - sig)))).astype(jnp.bfloat16)
        for h in range(tp):
            cols = slice(h * share, (h + 1) * share)
            tg_part[h, rows, 0:share] = (
                dot_nt(grad_gate, w_gate[cols, :]) + dot_nt(grad_up, w_up[cols, :])
            ).astype(jnp.bfloat16)
            tg_part[h, rows, share : share + LANES] = score

        @pl.when(k >= 2)
        def _():
            x_start(3, k)

    x_start(3, jnp.int32(1))
    x_start(3, jnp.int32(0))
    reduce_rows(3, jnp.int32(ep - 1))
    reduce_rows(3, jnp.int32(1))
    reduce_rows(3, jnp.int32(0))

    @pl.loop(1, ep)
    def _(k):
        z_copy(2, k).wait_recv()

    out_ref[...] = (dot_nn(unpack_ref[...], out_home[...]) * weight).astype(jnp.bfloat16)

    @pl.loop(1, ep)
    def _(k):
        z_copy(3, k).wait_recv()

    token_grad_ref[...] = (
        dot_nn(unpack_ref[...], tg_home[:, 0:share]) * weight
    ).astype(jnp.bfloat16)
    router_ref[...] = router_ref[...] * dot_nn(
        unpack_ref[...], tg_home[:, share : share + LANES]
    )

    @pl.loop(1, owner_count)
    def _(o):
        table_copy(o).wait_send()

    for kind in range(4):
        if kind < 2:
            near_copy(kind).wait_send()

        @pl.loop(2 if kind < 2 else 1, ep)
        def _(k):
            z_copy(kind, k).wait_send()

        @pl.loop(2 if kind < 2 else 0, ep)
        def _(k):
            for j in range(1, tp):
                x_copy(kind, k, j).wait_send()


def copy_kernel(a_in, b_in, c_in, a_out, b_out, c_out):
    a_out[...] = a_in[...]
    b_out[...] = b_in[...]
    c_out[...] = c_in[...]


def shards(logits, routes, owner, tokens, out_grad, resp_lengths, w_gate, w_up, w_down):
    tok_count, width = tokens.shape
    top = routes.shape[1]
    ep = lax.axis_size("ep")
    tp = lax.axis_size("tp")
    sp = lax.axis_size("sp")
    owner_count = ep * sp
    assert w_gate.shape[0] == 1 and ep >= 4 and ep & (ep - 1) == 0
    hidden_width = w_gate.shape[2]
    per = 2 * tok_count // ep
    slots = ep * per
    share = width // tp
    vmem = pl.BlockSpec(memory_space=pltpu.VMEM)
    anywhere = pl.BlockSpec(memory_space=pl.ANY)
    bf16 = jnp.bfloat16
    out_shape = (
        jax.ShapeDtypeStruct((tok_count, share), bf16),
        jax.ShapeDtypeStruct((tok_count, share), bf16),
        jax.ShapeDtypeStruct((tok_count, logits.shape[1]), jnp.float32),
    )
    results = pl.pallas_call(
        functools.partial(layer_kernel, ep, tp, sp, per),
        out_shape=out_shape,
        in_specs=[vmem] * 4 + [anywhere] * 5,
        out_specs=(vmem, vmem, vmem),
        scratch_shapes=[
            pltpu.VMEM((owner_count, 3 * top, tok_count), jnp.float32),
            pltpu.VMEM((slots, tok_count), bf16),
            pltpu.VMEM((slots, tok_count), bf16),
            pltpu.VMEM((tok_count, slots), bf16),
            pltpu.VMEM((tok_count, width), bf16),
            pltpu.VMEM((tok_count, width), bf16),
            pltpu.VMEM((width, hidden_width), bf16),
            pltpu.VMEM((width, hidden_width), bf16),
            pltpu.VMEM((hidden_width, width), bf16),
            pltpu.VMEM((ep, per, share), bf16),
            pltpu.VMEM((ep, per, share), bf16),
            pltpu.VMEM((tp, per, share), bf16),
            pltpu.VMEM((tp, per, share), bf16),
            pltpu.VMEM((tp, slots, share), bf16),
            pltpu.VMEM((tp, slots, share), bf16),
            pltpu.VMEM((slots, hidden_width), jnp.float32),
            pltpu.VMEM((slots, hidden_width), jnp.float32),
            pltpu.VMEM((slots, hidden_width), bf16),
            pltpu.VMEM((tp, slots, share), bf16),
            pltpu.VMEM((tp - 1, slots, share), bf16),
            pltpu.VMEM((slots, share), bf16),
            pltpu.VMEM((slots, share), bf16),
            pltpu.VMEM((tp, slots, share + LANES), bf16),
            pltpu.VMEM((tp - 1, slots, share + LANES), bf16),
            pltpu.VMEM((slots, share + LANES), bf16),
            pltpu.VMEM((slots, share + LANES), bf16),
            pltpu.SemaphoreType.DMA((5,)),
            pltpu.SemaphoreType.DMA((owner_count,)),
            pltpu.SemaphoreType.DMA((owner_count,)),
            pltpu.SemaphoreType.DMA((4, ep)),
            pltpu.SemaphoreType.DMA((4, ep)),
            pltpu.SemaphoreType.DMA((4, ep * tp)),
            pltpu.SemaphoreType.DMA((4, ep * tp)),
        ],
        compiler_params=pltpu.CompilerParams(
            collective_id=0, has_side_effects=True, vmem_limit_bytes=56 * 1024 * 1024
        ),
        cost_estimate=pl.CostEstimate(
            flops=12 * slots * width * hidden_width,
            bytes_accessed=6 * width * hidden_width + 6 * tok_count * width,
            transcendentals=2 * slots * hidden_width,
        ),
        name="expert_layer",
    )(
        logits,
        routes.T,
        owner.reshape(1, tok_count),
        resp_lengths.reshape(1, 1),
        tokens,
        out_grad,
        w_gate,
        w_up,
        w_down,
    )
    return pl.pallas_call(
        copy_kernel,
        out_shape=out_shape,
        in_specs=[vmem] * 3,
        out_specs=(vmem,) * 3,
        name="hand_over",
    )(*results)


def solution(mesh):
    in_specs = (
        P(("groups", "ep", "sp"), None),
        P(("groups", "ep", "sp"), None),
        P(("groups", "ep", "sp")),
        P(("groups", "ep", "sp"), None),
        P(("groups", "ep", "sp"), None),
        P(("groups", "ep", "sp")),
        P("ep", None, "tp"),
        P("ep", None, "tp"),
        P("ep", "tp", None),
    )
    out_specs = (
        P(("groups", "ep", "sp"), "tp"),
        P(("groups", "ep", "sp"), "tp"),
        P(("groups", "ep", "sp"), None),
    )
    return jax.shard_map(shards, mesh=mesh, in_specs=in_specs, out_specs=out_specs, check_vma=False)
```
